256 devices in a mesh: outer: 8 (over x, y_lo), inner: 32 (over y_hi, z, core).
Axes of the slice: x: 4, y: 4 (y_hi: 2, y_lo: 2; y = y_hi * 2 + y_lo), z: 8, core: 2. Of those that a mesh axis runs over, the one named last changes fastest.
Arguments:
- queries: bfloat16 [131072, 1024], P(('outer', 'inner')), may hold values from -6 to 6
- keys: bfloat16 [131072, 128], P(('outer', 'inner')), may hold values from -6 to 6
- values: bfloat16 [131072, 128], P(('outer', 'inner')), may hold values from -6 to 6
- grad_out: bfloat16 [131072, 1024], P(('outer', 'inner')), may hold values from -6 to 6
- turn_ids: int32 [131072], P(('outer', 'inner')), may hold values from 0 to 255, never falling along the last dimension, each value on 1 to 2048 neighbouring positions
- tool_spans: int32 [128, 2], replicated, may hold values from 0 to 131072, as said below
Outputs:
- grad_queries: bfloat16 [131072, 1024], P(('outer', 'inner'))
- grad_keys: bfloat16 [131072, 128], P(('outer', 'inner'))
- grad_values: bfloat16 [131072, 128], P(('outer', 'inner'))
The draws below stay inside these ranges and needn't reach their ends.
Inputs may be any that keep to these rules, and one draw needn't show every extreme that they name: `tool_spans`: rows are sorted and disjoint; each span has at least one position.
All inputs are finite; a program needn't handle non-finite values.
Results may differ from the reference program's by a relative error of at most 0.025.
Values may be sent and summed in bfloat16 or wider, within the bound.
A program may use at most 64 MiB of HBM per device.

```python
import math
import jax
import jax.numpy as jnp
import numpy as np
from jax import lax

HEADS = 8
HEAD_DIM = 128
TOK_DEV = 512
TOKENS = 131072
SPANS = 128


def draw_keys(key, part):
    key = jax.random.fold_in(key, 1)
    sample = jnp.clip(jax.random.normal(key, (TOKENS, HEAD_DIM), jnp.float32), -6.0, 6.0)
    return sample.astype(jnp.bfloat16)


def draw_queries(key, part):
    key = jax.random.fold_in(key, 2)
    sample = jnp.clip(jax.random.normal(key, (TOKENS, HEADS * HEAD_DIM), jnp.float32), -6.0, 6.0)
    return sample.astype(jnp.bfloat16)


def draw_tool_spans(key, part):
    key = jax.random.fold_in(key, 3)
    start_key, length_key = jax.random.split(key)
    slot_len = 2 * TOK_DEV
    slot_start = jnp.arange(SPANS, dtype=jnp.int32) * slot_len
    offset = jax.random.randint(start_key, (SPANS,), 0, slot_len // 2)
    length = jax.random.randint(length_key, (SPANS,), max(1, slot_len // 8), TOK_DEV + 1)
    starts = slot_start + offset
    return jnp.stack([starts, starts + length], axis=1).astype(jnp.int32)


def steps_of(key, extent, pieces, low, high):
    factor_of, own = 1.0, jax.random.fold_in(key, 6)
    for axis_at, shards_of in pieces:
        heights = jnp.exp(jax.random.uniform(jax.random.fold_in(own, axis_at), (shards_of,), jnp.float32, low / len(pieces), high / len(pieces)))
        factor_of = factor_of * jnp.repeat(heights, extent[axis_at] // shards_of).reshape([-1 if axis == axis_at else 1 for axis in range(len(extent))])
    return factor_of


def length_profile(count, total, most, lean):
    portions = [(1 << 20) // math.isqrt(standing ** lean) + 1 for standing in range(2, count + 1)]
    surplus, holding = total - most - (count - 1), [1] * (count - 1)
    while surplus > 0:
        free = [i for i in range(count - 1) if holding[i] < most]
        pool, budget = sum([portions[i] for i in free]), surplus
        for i in free:
            extra = min(most - holding[i], max(1, budget * portions[i] // pool), surplus)
            holding[i] = holding[i] + extra
            surplus = surplus - extra
    return np.array([most] + holding)


def ragged_sizes(key, number_of, total, most, slope):
    if number_of == 2:
        one = jax.random.randint(key, (), max(1, total - most), min(most, total - 1) + 1)
        return jnp.stack([one, total - one])
    tallies = jnp.asarray(length_profile(number_of, total, most, slope), jnp.int32)
    couples = (number_of - 1) // 2
    donor, receiver = tallies[1:1 + 2 * couples:2], tallies[2:2 + 2 * couples:2]
    room = jnp.minimum(donor - 1, most - receiver)
    moved = jax.random.randint(jax.random.fold_in(key, 1), (couples,), 0, 1 << 20) % (room + 1)
    tallies = tallies.at[1:1 + 2 * couples:2].set(donor - moved).at[2:2 + 2 * couples:2].set(receiver + moved)
    return tallies[jax.random.permutation(jax.random.fold_in(key, 2), number_of)]


def noise(key, extent, spread, bound, shards=(), held_as=jnp.bfloat16):
    entries = spread * jax.random.normal(key, extent, jnp.float32)
    if shards:
        entries = entries * steps_of(key, extent, shards, -0.22, 0.18)
    return jnp.clip(entries, -bound, bound).astype(held_as)


def setup_inputs(seed: int = 0) -> dict:
    splits = jax.random.split(jax.random.key(seed), 7)
    return {
        "queries": draw_queries(jax.random.fold_in(splits[6], 71), 0),
        "keys": draw_keys(jax.random.fold_in(splits[6], 71), 0),
        "values": noise(splits[2], (TOKENS, HEAD_DIM), 1.0, 6.0, ((0, 256),)),
        "grad_out": noise(splits[3], (TOKENS, HEADS * HEAD_DIM), 1.0, 6.0, ((0, 256),)),
        "turn_ids": jnp.searchsorted(jnp.cumsum(ragged_sizes(splits[4], TOKENS // TOK_DEV, TOKENS, 4 * TOK_DEV, 2)), jnp.arange(TOKENS), side="right").astype(jnp.int32),
        "tool_spans": draw_tool_spans(jax.random.fold_in(splits[6], 71), 0),
    }


def reference(queries, keys, values, grad_out, turn_ids, tool_spans):
    reach = 4 * TOK_DEV
    score_scale = HEAD_DIM ** -0.5
    positions = jnp.arange(TOKENS, dtype=jnp.int32)
    in_tool = jnp.any((positions[:, None] >= tool_spans[None, :, 0]) & (positions[:, None] < tool_spans[None, :, 1]), axis=1)
    key_pad = jnp.concatenate([jnp.zeros((reach, HEAD_DIM), keys.dtype), keys])
    value_pad = jnp.concatenate([jnp.zeros((reach, HEAD_DIM), values.dtype), values])
    turn_pad = jnp.concatenate([jnp.zeros((reach,), jnp.int32), turn_ids])
    tool_pad = jnp.concatenate([jnp.zeros((reach,), bool), in_tool])

    def block_step(carry, block_index):
        grad_key_sum, grad_value_sum = carry
        first = (block_index * TOK_DEV).astype(jnp.int32)
        width_all = reach + TOK_DEV
        query_rows = lax.dynamic_slice_in_dim(queries, first, TOK_DEV, 0).reshape(TOK_DEV, HEADS, HEAD_DIM).astype(jnp.float32)
        cotangent = lax.dynamic_slice_in_dim(grad_out, first, TOK_DEV, 0).reshape(TOK_DEV, HEADS, HEAD_DIM).astype(jnp.float32)
        key_window = lax.dynamic_slice_in_dim(key_pad, first, width_all, 0).astype(jnp.float32)
        value_window = lax.dynamic_slice_in_dim(value_pad, first, width_all, 0).astype(jnp.float32)
        turn_query = lax.dynamic_slice_in_dim(turn_ids, first, TOK_DEV, 0)
        turn_key = lax.dynamic_slice_in_dim(turn_pad, first, width_all, 0)
        tool_key = lax.dynamic_slice_in_dim(tool_pad, first, width_all, 0)
        query_pos = first + jnp.arange(TOK_DEV, dtype=jnp.int32)
        key_pos = first - reach + jnp.arange(width_all, dtype=jnp.int32)
        distance = query_pos[:, None] - key_pos[None, :]
        visible = (key_pos[None, :] >= 0) & (distance >= 0) & (distance < reach)
        visible = visible & (jnp.logical_not(tool_key)[None, :] | (turn_key[None, :] == turn_query[:, None]))
        scores = jnp.einsum("thd,kd->htk", query_rows, key_window) * score_scale
        masked = jnp.where(visible[None], scores, -jnp.inf)
        row_top = jnp.max(masked, axis=-1, keepdims=True)
        log_total = row_top + jnp.log(jnp.sum(jnp.exp(masked - row_top), axis=-1, keepdims=True))
        probs = jnp.exp(masked - log_total)
        probs_low = lax.optimization_barrier(probs.astype(jnp.bfloat16)).astype(jnp.float32)
        attended = jnp.einsum("htk,kd->thd", probs_low, value_window).astype(jnp.bfloat16)
        attended = lax.optimization_barrier(attended).astype(jnp.float32)
        delta = jnp.sum(cotangent * attended, axis=-1)
        dprobs = jnp.einsum("thd,kd->htk", cotangent, value_window)
        dscores = (probs * (dprobs - jnp.transpose(delta)[:, :, None])).astype(jnp.bfloat16)
        dscores = lax.optimization_barrier(dscores).astype(jnp.float32)
        grad_query = (jnp.einsum("htk,kd->thd", dscores, key_window) * score_scale).astype(jnp.bfloat16)
        grad_key_part = jnp.einsum("htk,thd->kd", dscores, query_rows) * score_scale
        grad_value_part = jnp.einsum("htk,thd->kd", probs_low, cotangent)
        grad_key_sum = lax.dynamic_update_slice_in_dim(grad_key_sum, lax.dynamic_slice_in_dim(grad_key_sum, first, width_all, 0) + grad_key_part, first, 0)
        grad_value_sum = lax.dynamic_update_slice_in_dim(grad_value_sum, lax.dynamic_slice_in_dim(grad_value_sum, first, width_all, 0) + grad_value_part, first, 0)
        return (grad_key_sum, grad_value_sum), grad_query.reshape(TOK_DEV, HEADS * HEAD_DIM)

    zeros_pad = jnp.zeros((TOKENS + reach, HEAD_DIM), jnp.float32)
    (grad_key_sum, grad_value_sum), grad_blocks = lax.scan(block_step, (zeros_pad, zeros_pad), jnp.arange(TOKENS // TOK_DEV, dtype=jnp.int32))
    grad_queries = grad_blocks.reshape(TOKENS, HEADS * HEAD_DIM)
    return grad_queries, grad_key_sum[reach:].astype(jnp.bfloat16), grad_value_sum[reach:].astype(jnp.bfloat16)
```

```python
import functools

import jax
import jax.numpy as jnp
from jax import lax
from jax.experimental import pallas as pl
from jax.experimental.pallas import tpu as pltpu
from jax.sharding import PartitionSpec as P

F32 = jnp.float32
BF16 = jnp.bfloat16
LOG2E = 1.4426950408889634
HIDE = 16384.0
NT = (((1,), (1,)), ((), ()))
BACK = 4


def dot(a, b):
    return jnp.dot(a, b, preferred_element_type=F32)


def dot_nt(a, b):
    return lax.dot_general(a, b, NT, preferred_element_type=F32)


def regions(hops, rows):
    half = rows // 2
    if hops == 0:
        return ((0, half, 0, half), (0, rows, half, half))
    if hops == BACK:
        return ((0, rows, 0, half), (half, half, half, half))
    return ((0, rows, 0, rows),)


def one_hot_rows(turn, width):
    row = lax.broadcasted_iota(jnp.int32, (width, turn.shape[1]), 0)
    high = jnp.where(row < 16, turn >> 4, -1)
    low = jnp.where((row >= 16) & (row < 32), (turn & 15) + 16, -1)
    return (row == high) | (row == low), row == 32


def kernel(
    inner_count,
    device_count,
    q_hbm,
    do_hbm,
    k_ref,
    v_ref,
    t_ref,
    sp_ref,
    gq_ref,
    gk_ref,
    gv_ref,
    q_s,
    do_s,
    kw,
    vw,
    ww,
    kc,
    kt,
    qc,
    es,
    ds,
    ms,
    ls,
    dl,
    gq_acc,
    gk_acc,
    gv_acc,
    gk_out,
    gv_out,
    gk_in,
    gv_in,
    in_sems,
    send_sems,
    recv_sems,
    gsend_sems,
    grecv_sems,
):
    rows, width = k_ref.shape
    heads = q_hbm.shape[1] // width
    scale = width ** (-0.5)
    to_exp2 = scale * LOG2E
    me = lax.axis_index("outer") * inner_count + lax.axis_index("inner")
    right = lax.rem(me + 1, device_count)
    left = lax.rem(me + device_count - 1, device_count)
    right_id = (right // inner_count, lax.rem(right, inner_count))
    left_id = (left // inner_count, lax.rem(left, inner_count))

    q_copy = pltpu.make_async_copy(q_hbm, q_s, in_sems.at[0])
    do_copy = pltpu.make_async_copy(do_hbm, do_s, in_sems.at[1])
    q_copy.start()
    do_copy.start()

    barrier = pltpu.get_barrier_semaphore()
    for neighbour in (left_id, right_id):
        pl.semaphore_signal(
            barrier, inc=1, device_id=neighbour, device_id_type=pl.DeviceIdType.MESH
        )

    turn = t_ref[...]
    pos = me * rows + lax.broadcasted_iota(jnp.int32, (1, rows), 1)
    inside = (pos >= sp_ref[:, 0:1]) & (pos < sp_ref[:, 1:2])
    tool = jnp.max(jnp.where(inside, 1.0, 0.0), axis=0, keepdims=True)
    ww[0] = jnp.where(tool > 0.5, turn, -1)

    pl.semaphore_wait(barrier, 2)

    def hop_copies(hop):
        parts = (
            (k_ref if hop == 1 else kw.at[hop - 2], kw.at[hop - 1]),
            (ww.at[hop - 1], ww.at[hop]),
            (v_ref if hop == 1 else vw.at[hop - 2], vw.at[hop - 1]),
        )
        return [
            pltpu.make_async_remote_copy(
                src_ref=src,
                dst_ref=dst,
                send_sem=send_sems.at[hop - 1, at],
                recv_sem=recv_sems.at[hop - 1, at],
                device_id=right_id,
                device_id_type=pl.DeviceIdType.MESH,
            )
            for at, (src, dst) in enumerate(parts)
        ]

    copies = {hop: hop_copies(hop) for hop in range(1, BACK + 1)}
    for copy in copies[1]:
        copy.start()

    def key_block(hops):
        return k_ref if hops == 0 else kw.at[hops - 1]

    def value_block(hops):
        return v_ref if hops == 0 else vw.at[hops - 1]

    hit, one = one_hot_rows(turn, width)
    qc[...] = jnp.transpose(jnp.where(hit | one, 1.0, 0.0)).astype(BF16)

    def prepare(hops):
        w = ww[hops]
        if hops:
            w = jnp.where(me >= hops, w, 1024)
        hit, one = one_hot_rows(w, width)
        code = jnp.where(hit, HIDE, jnp.where(one, -2.0 * HIDE, 0.0))
        code = jnp.where(w >= 0, code, 0.0)
        kc[hops] = jnp.transpose(code).astype(BF16)
        kt[hops] = jnp.transpose(key_block(hops)[...].astype(F32)).astype(BF16)

    def score_part(hops, h, part):
        k0, kn, r0, rn = part
        cols = pl.ds(pl.multiple_of(h * width, width), width)
        k_rows, q_rows = pl.ds(k0, kn), pl.ds(r0, rn)
        keyed = jnp.concatenate([key_block(hops)[k_rows, :], kc[hops, k_rows, :]], axis=1)
        asked = jnp.concatenate([q_s[q_rows, cols], qc[q_rows, :]], axis=1)
        s = dot_nt(keyed, asked)
        dp = dot_nt(value_block(hops)[k_rows, :], do_s[q_rows, cols])
        if hops in (0, BACK):
            key_at = k0 + lax.broadcasted_iota(jnp.int32, (kn, rn), 0)
            row_at = r0 + lax.broadcasted_iota(jnp.int32, (kn, rn), 1)
            seen = key_at <= row_at if hops == 0 else key_at > row_at
            s = jnp.where(seen, s, -2.0 * HIDE)
        top = jnp.max(s, axis=0, keepdims=True) * to_exp2
        if hops:
            before = ms[hops - 1, h, :, q_rows]
            top = jnp.maximum(before, top)
        e = jnp.exp2(s * to_exp2 - top)
        total = jnp.sum(e, axis=0, keepdims=True)
        inner = jnp.sum(e * dp, axis=0, keepdims=True)
        if hops:
            fade = jnp.exp2(before - top)
            total = total + ls[h, :, q_rows] * fade
            inner = inner + dl[h, :, q_rows] * fade
        ms[hops, h, :, q_rows] = top
        ls[h, :, q_rows] = total
        dl[h, :, q_rows] = inner
        es[hops, h, k_rows, q_rows] = e.astype(BF16)
        ds[hops, h, k_rows, q_rows] = dp.astype(BF16)

    def over_heads(step, unroll):
        def body(i, carry):
            for u in range(unroll):
                step(i * unroll + u)
            return carry

        lax.fori_loop(0, heads // unroll, body, 0)

    def score_block(hops):
        def step(h):
            for part in regions(hops, rows):
                score_part(hops, h, part)

        over_heads(step, 2)

    prepare(0)
    q_copy.wait()
    do_copy.wait()
    score_block(0)
    for hops in range(1, BACK + 1):
        for copy in copies[hops]:
            copy.wait_recv()
        if hops < BACK:
            for copy in copies[hops + 1]:
                copy.start()
        prepare(hops)
        score_block(hops)

    def finish(h):
        share = 1.0 / ls[h]
        last = ms[BACK, h]
        dl[h] = dl[h] * share
        for hops in range(BACK + 1):
            ms[hops, h] = jnp.exp2(ms[hops, h] - last) * share

    over_heads(finish, 1)

    def grad_part(hops, h, part):
        k0, kn, r0, rn = part
        cols = pl.ds(pl.multiple_of(h * width, width), width)
        k_rows, q_rows = pl.ds(k0, kn), pl.ds(r0, rn)
        p = es[hops, h, k_rows, q_rows].astype(F32) * ms[hops, h, :, q_rows]
        g = p * (ds[hops, h, k_rows, q_rows].astype(F32) - dl[h, :, q_rows])
        p = p.astype(BF16)
        g = g.astype(BF16)
        gk_acc[k_rows, :] += dot(g, q_s[q_rows, cols])
        gv_acc[k_rows, :] += dot(p, do_s[q_rows, cols])
        gq = dot(kt[hops, :, k_rows], g)
        if hops == BACK:
            gq_acc[h, :, q_rows] = gq
        else:
            gq_acc[h, :, q_rows] += gq

    def grad_copies(step):
        return [
            pltpu.make_async_remote_copy(
                src_ref=src.at[step],
                dst_ref=dst.at[step],
                send_sem=gsend_sems.at[step, at],
                recv_sem=grecv_sems.at[step, at],
                device_id=left_id,
                device_id_type=pl.DeviceIdType.MESH,
            )
            for at, (src, dst) in enumerate(((gk_out, gk_in), (gv_out, gv_in)))
        ]

    returns = [grad_copies(step) for step in range(BACK)]

    for step in range(BACK + 1):
        hops = BACK - step
        gk_acc[...] = jnp.zeros_like(gk_acc)
        gv_acc[...] = jnp.zeros_like(gv_acc)

        def grad_step(h):
            for part in regions(hops, rows):
                grad_part(hops, h, part)

        over_heads(grad_step, 2)
        if hops == 0:
            for h in range(heads):
                gq_ref[:, h * width : (h + 1) * width] = (
                    jnp.transpose(gq_acc[h] * scale)
                ).astype(BF16)
        gk = gk_acc[...]
        gv = gv_acc[...]
        if step:
            for copy in returns[step - 1]:
                copy.wait_recv()
            gk = gk + gk_in[step - 1].astype(F32)
            gv = gv + gv_in[step - 1].astype(F32)
        if hops:
            gk_out[step] = gk.astype(BF16)
            gv_out[step] = gv.astype(BF16)
            for copy in returns[step]:
                copy.start()
        else:
            gk_ref[...] = (gk * scale).astype(BF16)
            gv_ref[...] = gv.astype(BF16)

    for hop in range(1, BACK + 1):
        for copy in copies[hop]:
            copy.wait_send()
    for step in range(BACK):
        for copy in returns[step]:
            copy.wait_send()


def on_device(inner_count, device_count, queries, keys, values, grad_out, turn_ids, tool_spans):
    rows, width = keys.shape
    heads = queries.shape[1] // width
    vmem = pl.BlockSpec(memory_space=pltpu.VMEM)
    hbm = pl.BlockSpec(memory_space=pl.ANY)
    block = (rows, width)
    dma = pltpu.SemaphoreType.DMA
    flops = 2 * 5 * heads * rows * (BACK + 1) * rows * width
    return pl.pallas_call(
        functools.partial(kernel, inner_count, device_count),
        out_shape=(
            jax.ShapeDtypeStruct(queries.shape, BF16),
            jax.ShapeDtypeStruct(keys.shape, BF16),
            jax.ShapeDtypeStruct(values.shape, BF16),
        ),
        in_specs=[hbm, hbm, vmem, vmem, vmem, vmem],
        out_specs=(vmem, vmem, vmem),
        scratch_shapes=[
            pltpu.VMEM(queries.shape, BF16),
            pltpu.VMEM(queries.shape, BF16),
            pltpu.VMEM((BACK,) + block, BF16),
            pltpu.VMEM((BACK,) + block, BF16),
            pltpu.VMEM((BACK + 1, 1, rows), jnp.int32),
            pltpu.VMEM((BACK + 1,) + block, BF16),
            pltpu.VMEM((BACK + 1, width, rows), BF16),
            pltpu.VMEM(block, BF16),
            pltpu.VMEM((BACK + 1, heads, rows, rows), BF16),
            pltpu.VMEM((BACK + 1, heads, rows, rows), BF16),
            pltpu.VMEM((BACK + 1, heads, 1, rows), F32),
            pltpu.VMEM((heads, 1, rows), F32),
            pltpu.VMEM((heads, 1, rows), F32),
            pltpu.VMEM((heads, width, rows), F32),
            pltpu.VMEM(block, F32),
            pltpu.VMEM(block, F32),
            pltpu.VMEM((BACK,) + block, BF16),
            pltpu.VMEM((BACK,) + block, BF16),
            pltpu.VMEM((BACK,) + block, BF16),
            pltpu.VMEM((BACK,) + block, BF16),
            dma((2,)),
            dma((BACK, 3)),
            dma((BACK, 3)),
            dma((BACK, 2)),
            dma((BACK, 2)),
        ],
        compiler_params=pltpu.CompilerParams(
            collective_id=0, has_side_effects=True, vmem_limit_bytes=60 * 1024 * 1024
        ),
        cost_estimate=pl.CostEstimate(
            flops=flops, bytes_accessed=8 * 1024 * 1024, transcendentals=0
        ),
    )(queries, grad_out, keys, values, turn_ids.reshape(1, rows), tool_spans)


def solution(mesh):
    placed = (
        P(("outer", "inner"), None),
        P(("outer", "inner"), None),
        P(("outer", "inner"), None),
        P(("outer", "inner"), None),
        P(("outer", "inner")),
        P(),
    )
    return jax.shard_map(
        functools.partial(on_device, mesh.shape["inner"], mesh.size),
        mesh=mesh,
        in_specs=placed,
        out_specs=(
            P(("outer", "inner"), None),
            P(("outer", "inner"), None),
            P(("outer", "inner"), None),
        ),
        check_vma=False,
    )
```

```python
import functools

import jax
import jax.numpy as jnp
from jax import lax
from jax.experimental import pallas as pl
from jax.experimental.pallas import tpu as pltpu
from jax.sharding import PartitionSpec as P

F32 = jnp.float32
BF16 = jnp.bfloat16
LOG2E = 1.4426950408889634
HIDE = 16384.0
NT = (((1,), (1,)), ((), ()))
BACK = 4


def dot(a, b):
    return jnp.dot(a, b, preferred_element_type=F32)


def dot_nt(a, b):
    return lax.dot_general(a, b, NT, preferred_element_type=F32)


def regions(hops, rows):
    half = rows // 2
    if hops == 0:
        return ((0, half, 0, half), (0, rows, half, half))
    if hops == BACK:
        return ((0, rows, 0, half), (half, half, half, half))
    return ((0, rows, 0, rows),)


def one_hot_rows(turn, width):
    row = lax.broadcasted_iota(jnp.int32, (width, turn.shape[1]), 0)
    high = jnp.where(row < 16, turn >> 4, -1)
    low = jnp.where((row >= 16) & (row < 32), (turn & 15) + 16, -1)
    return (row == high) | (row == low), row == 32


def kernel(
    inner_count,
    device_count,
    q_hbm,
    do_hbm,
    k_ref,
    v_ref,
    t_ref,
    sp_ref,
    gq_ref,
    gk_ref,
    gv_ref,
    q_s,
    do_s,
    kw,
    vw,
    ww,
    kc,
    kt,
    qc,
    es,
    ds,
    ms,
    ls,
    dl,
    gq_acc,
    gk_acc,
    gv_acc,
    gk_out,
    gv_out,
    gk_in,
    gv_in,
    in_sems,
    send_sems,
    recv_sems,
    gsend_sems,
    grecv_sems,
):
    rows, width = k_ref.shape
    heads = q_hbm.shape[1] // width
    scale = width ** (-0.5)
    to_exp2 = scale * LOG2E
    me = lax.axis_index("outer") * inner_count + lax.axis_index("inner")
    right = lax.rem(me + 1, device_count)
    left = lax.rem(me + device_count - 1, device_count)
    right_id = (right // inner_count, lax.rem(right, inner_count))
    left_id = (left // inner_count, lax.rem(left, inner_count))

    q_copy = pltpu.make_async_copy(q_hbm, q_s, in_sems.at[0])
    do_copy = pltpu.make_async_copy(do_hbm, do_s, in_sems.at[1])
    q_copy.start()
    do_copy.start()

    barrier = pltpu.get_barrier_semaphore()
    for neighbour in (left_id, right_id):
        pl.semaphore_signal(
            barrier, inc=1, device_id=neighbour, device_id_type=pl.DeviceIdType.MESH
        )

    turn = t_ref[...]
    pos = me * rows + lax.broadcasted_iota(jnp.int32, (1, rows), 1)
    count = sp_ref.shape[1]
    first = jnp.transpose(jnp.broadcast_to(sp_ref[0:1, :], (8, count)))[:, 0:1]
    after = jnp.transpose(jnp.broadcast_to(sp_ref[1:2, :], (8, count)))[:, 0:1]
    inside = (pos >= first) & (pos < after)
    tool = jnp.max(jnp.where(inside, 1.0, 0.0), axis=0, keepdims=True)
    ww[0] = jnp.where(tool > 0.5, turn, -1)

    pl.semaphore_wait(barrier, 2)

    def hop_copies(hop):
        parts = (
            (k_ref if hop == 1 else kw.at[hop - 2], kw.at[hop - 1]),
            (ww.at[hop - 1], ww.at[hop]),
            (v_ref if hop == 1 else vw.at[hop - 2], vw.at[hop - 1]),
        )
        return [
            pltpu.make_async_remote_copy(
                src_ref=src,
                dst_ref=dst,
                send_sem=send_sems.at[hop - 1, at],
                recv_sem=recv_sems.at[hop - 1, at],
                device_id=right_id,
                device_id_type=pl.DeviceIdType.MESH,
            )
            for at, (src, dst) in enumerate(parts)
        ]

    copies = {hop: hop_copies(hop) for hop in range(1, BACK + 1)}
    for copy in copies[1]:
        copy.start()

    def key_block(hops):
        return k_ref if hops == 0 else kw.at[hops - 1]

    def value_block(hops):
        return v_ref if hops == 0 else vw.at[hops - 1]

    hit, one = one_hot_rows(turn, width)
    qc[...] = jnp.transpose(jnp.where(hit | one, 1.0, 0.0)).astype(BF16)

    def prepare(hops):
        w = ww[hops]
        if hops:
            w = jnp.where(me >= hops, w, 1024)
        hit, one = one_hot_rows(w, width)
        code = jnp.where(hit, HIDE, jnp.where(one, -2.0 * HIDE, 0.0))
        code = jnp.where(w >= 0, code, 0.0)
        kc[hops] = jnp.transpose(code).astype(BF16)
        kt[hops] = jnp.transpose(key_block(hops)[...].astype(F32)).astype(BF16)

    def score_part(hops, h, part):
        k0, kn, r0, rn = part
        cols = pl.ds(pl.multiple_of(h * width, width), width)
        k_rows, q_rows = pl.ds(k0, kn), pl.ds(r0, rn)
        keyed = jnp.concatenate([key_block(hops)[k_rows, :], kc[hops, k_rows, :]], axis=1)
        asked = jnp.concatenate([q_s[q_rows, cols], qc[q_rows, :]], axis=1)
        s = dot_nt(keyed, asked)
        dp = dot_nt(value_block(hops)[k_rows, :], do_s[q_rows, cols])
        if hops in (0, BACK):
            key_at = k0 + lax.broadcasted_iota(jnp.int32, (kn, rn), 0)
            row_at = r0 + lax.broadcasted_iota(jnp.int32, (kn, rn), 1)
            seen = key_at <= row_at if hops == 0 else key_at > row_at
            s = jnp.where(seen, s, -2.0 * HIDE)
        top = jnp.max(s, axis=0, keepdims=True) * to_exp2
        if hops:
            before = ms[hops - 1, h, :, q_rows]
            top = jnp.maximum(before, top)
        e = jnp.exp2(s * to_exp2 - top)
        total = jnp.sum(e, axis=0, keepdims=True)
        inner = jnp.sum(e * dp, axis=0, keepdims=True)
        if hops:
            fade = jnp.exp2(before - top)
            total = total + ls[h, :, q_rows] * fade
            inner = inner + dl[h, :, q_rows] * fade
        ms[hops, h, :, q_rows] = top
        ls[h, :, q_rows] = total
        dl[h, :, q_rows] = inner
        es[hops, h, k_rows, q_rows] = e.astype(BF16)
        ds[hops, h, k_rows, q_rows] = dp.astype(BF16)

    def over_heads(step, unroll):
        def body(i, carry):
            for u in range(unroll):
                step(i * unroll + u)
            return carry

        lax.fori_loop(0, heads // unroll, body, 0)

    def score_block(hops):
        def step(h):
            for part in regions(hops, rows):
                score_part(hops, h, part)

        over_heads(step, 8)

    prepare(0)
    q_copy.wait()
    do_copy.wait()
    score_block(0)
    for hops in range(1, BACK + 1):
        for copy in copies[hops]:
            copy.wait_recv()
        if hops < BACK:
            for copy in copies[hops + 1]:
                copy.start()
        prepare(hops)
        score_block(hops)

    def finish(h):
        share = 1.0 / ls[h]
        last = ms[BACK, h]
        dl[h] = dl[h] * share
        for hops in range(BACK + 1):
            ms[hops, h] = jnp.exp2(ms[hops, h] - last) * share

    over_heads(finish, 1)

    def grad_part(hops, h, part):
        k0, kn, r0, rn = part
        cols = pl.ds(pl.multiple_of(h * width, width), width)
        k_rows, q_rows = pl.ds(k0, kn), pl.ds(r0, rn)
        p = es[hops, h, k_rows, q_rows].astype(F32) * ms[hops, h, :, q_rows]
        g = p * (ds[hops, h, k_rows, q_rows].astype(F32) - dl[h, :, q_rows])
        p = p.astype(BF16)
        g = g.astype(BF16)
        gk_acc[k_rows, :] += dot(g, q_s[q_rows, cols])
        gv_acc[k_rows, :] += dot(p, do_s[q_rows, cols])
        gq = dot(kt[hops, :, k_rows], g)
        if hops == BACK:
            gq_acc[h, :, q_rows] = gq
        else:
            gq_acc[h, :, q_rows] += gq

    def grad_copies(step):
        return [
            pltpu.make_async_remote_copy(
                src_ref=src.at[step],
                dst_ref=dst.at[step],
                send_sem=gsend_sems.at[step, at],
                recv_sem=grecv_sems.at[step, at],
                device_id=left_id,
                device_id_type=pl.DeviceIdType.MESH,
            )
            for at, (src, dst) in enumerate(((gk_out, gk_in), (gv_out, gv_in)))
        ]

    returns = [grad_copies(step) for step in range(BACK)]

    for step in range(BACK + 1):
        hops = BACK - step
        gk_acc[...] = jnp.zeros_like(gk_acc)
        gv_acc[...] = jnp.zeros_like(gv_acc)

        def grad_step(h):
            for part in regions(hops, rows):
                grad_part(hops, h, part)

        over_heads(grad_step, 4)
        if hops == 0:
            for h in range(heads):
                gq_ref[:, h * width : (h + 1) * width] = (
                    jnp.transpose(gq_acc[h] * scale)
                ).astype(BF16)
        gk = gk_acc[...]
        gv = gv_acc[...]
        if step:
            for copy in returns[step - 1]:
                copy.wait_recv()
            gk = gk + gk_in[step - 1].astype(F32)
            gv = gv + gv_in[step - 1].astype(F32)
        if hops:
            gk_out[step] = gk.astype(BF16)
            gv_out[step] = gv.astype(BF16)
            for copy in returns[step]:
                copy.start()
        else:
            gk_ref[...] = (gk * scale).astype(BF16)
            gv_ref[...] = gv.astype(BF16)

    for hop in range(1, BACK + 1):
        for copy in copies[hop]:
            copy.wait_send()
    for step in range(BACK):
        for copy in returns[step]:
            copy.wait_send()


def hand_out(gq_in, gk_in, gv_in, gq_ref, gk_ref, gv_ref):
    gq_ref[...] = gq_in[...]
    gk_ref[...] = gk_in[...]
    gv_ref[...] = gv_in[...]


def on_device(inner_count, device_count, queries, keys, values, grad_out, turn_ids, tool_spans):
    rows, width = keys.shape
    heads = queries.shape[1] // width
    vmem = pl.BlockSpec(memory_space=pltpu.VMEM)
    hbm = pl.BlockSpec(memory_space=pl.ANY)
    block = (rows, width)
    dma = pltpu.SemaphoreType.DMA
    flops = 2 * 5 * heads * rows * (BACK + 1) * rows * width
    parts = pl.pallas_call(
        functools.partial(kernel, inner_count, device_count),
        out_shape=(
            jax.ShapeDtypeStruct(queries.shape, BF16),
            jax.ShapeDtypeStruct(keys.shape, BF16),
            jax.ShapeDtypeStruct(values.shape, BF16),
        ),
        in_specs=[hbm, hbm, vmem, vmem, vmem, vmem],
        out_specs=(vmem, vmem, vmem),
        scratch_shapes=[
            pltpu.VMEM(queries.shape, BF16),
            pltpu.VMEM(queries.shape, BF16),
            pltpu.VMEM((BACK,) + block, BF16),
            pltpu.VMEM((BACK,) + block, BF16),
            pltpu.VMEM((BACK + 1, 1, rows), jnp.int32),
            pltpu.VMEM((BACK + 1,) + block, BF16),
            pltpu.VMEM((BACK + 1, width, rows), BF16),
            pltpu.VMEM(block, BF16),
            pltpu.VMEM((BACK + 1, heads, rows, rows), BF16),
            pltpu.VMEM((BACK + 1, heads, rows, rows), BF16),
            pltpu.VMEM((BACK + 1, heads, 1, rows), F32),
            pltpu.VMEM((heads, 1, rows), F32),
            pltpu.VMEM((heads, 1, rows), F32),
            pltpu.VMEM((heads, width, rows), F32),
            pltpu.VMEM(block, F32),
            pltpu.VMEM(block, F32),
            pltpu.VMEM((BACK,) + block, BF16),
            pltpu.VMEM((BACK,) + block, BF16),
            pltpu.VMEM((BACK,) + block, BF16),
            pltpu.VMEM((BACK,) + block, BF16),
            dma((2,)),
            dma((BACK, 3)),
            dma((BACK, 3)),
            dma((BACK, 2)),
            dma((BACK, 2)),
        ],
        compiler_params=pltpu.CompilerParams(
            collective_id=0, has_side_effects=True, vmem_limit_bytes=60 * 1024 * 1024
        ),
        cost_estimate=pl.CostEstimate(
            flops=flops, bytes_accessed=8 * 1024 * 1024, transcendentals=0
        ),
    )(queries, grad_out, keys, values, turn_ids.reshape(1, rows), tool_spans.T)
    return pl.pallas_call(
        hand_out,
        out_shape=tuple(jax.ShapeDtypeStruct(part.shape, part.dtype) for part in parts),
        in_specs=[vmem, vmem, vmem],
        out_specs=(vmem, vmem, vmem),
        scratch_shapes=[],
    )(*parts)


def solution(mesh):
    placed = (
        P(("outer", "inner"), None),
        P(("outer", "inner"), None),
        P(("outer", "inner"), None),
        P(("outer", "inner"), None),
        P(("outer", "inner")),
        P(),
    )
    return jax.shard_map(
        functools.partial(on_device, mesh.shape["inner"], mesh.size),
        mesh=mesh,
        in_specs=placed,
        out_specs=(
            P(("outer", "inner"), None),
            P(("outer", "inner"), None),
            P(("outer", "inner"), None),
        ),
        check_vma=False,
    )
```

```python
import functools

import jax
import jax.numpy as jnp
from jax import lax
from jax.experimental import pallas as pl
from jax.experimental.pallas import tpu as pltpu
from jax.sharding import PartitionSpec as P

F32 = jnp.float32
BF16 = jnp.bfloat16
LOG2E = 1.4426950408889634
HIDE = 16384.0
NT = (((1,), (1,)), ((), ()))
BACK = 4


def dot(a, b):
    return jnp.dot(a, b, preferred_element_type=F32)


def dot_nt(a, b):
    return lax.dot_general(a, b, NT, preferred_element_type=F32)


def regions(hops, rows):
    half = rows // 2
    if hops == 0:
        return ((0, half, 0, half), (0, rows, half, half))
    if hops == BACK:
        return ((0, rows, 0, half), (half, half, half, half))
    return ((0, rows, 0, rows),)


def one_hot_rows(turn, width):
    row = lax.broadcasted_iota(jnp.int32, (width, turn.shape[1]), 0)
    high = jnp.where(row < 16, turn >> 4, -1)
    low = jnp.where((row >= 16) & (row < 32), (turn & 15) + 16, -1)
    return (row == high) | (row == low), row == 32


def kernel(
    inner_count,
    device_count,
    q_hbm,
    do_hbm,
    k_ref,
    v_ref,
    t_ref,
    sp_ref,
    gq_ref,
    gk_ref,
    gv_ref,
    q_s,
    do_s,
    kw,
    vw,
    ww,
    kc,
    kt,
    qc,
    es,
    ds,
    ms,
    ls,
    dl,
    gq_acc,
    gk_acc,
    gv_acc,
    gk_out,
    gv_out,
    gk_in,
    gv_in,
    in_sems,
    send_sems,
    recv_sems,
    gsend_sems,
    grecv_sems,
):
    rows, width = k_ref.shape
    heads = q_hbm.shape[1] // width
    scale = width ** (-0.5)
    to_exp2 = scale * LOG2E
    me = lax.axis_index("outer") * inner_count + lax.axis_index("inner")
    right = lax.rem(me + 1, device_count)
    left = lax.rem(me + device_count - 1, device_count)
    right_id = (right // inner_count, lax.rem(right, inner_count))
    left_id = (left // inner_count, lax.rem(left, inner_count))

    q_copy = pltpu.make_async_copy(q_hbm, q_s, in_sems.at[0])
    do_copy = pltpu.make_async_copy(do_hbm, do_s, in_sems.at[1])
    q_copy.start()
    do_copy.start()

    barrier = pltpu.get_barrier_semaphore()
    for neighbour in (left_id, right_id):
        pl.semaphore_signal(
            barrier, inc=1, device_id=neighbour, device_id_type=pl.DeviceIdType.MESH
        )

    pl.semaphore_wait(barrier, 2)

    def hop_copies(hop):
        parts = (
            (k_ref if hop == 1 else kw.at[hop - 2], kw.at[hop - 1]),
            (ww.at[hop - 1], ww.at[hop]),
            (v_ref if hop == 1 else vw.at[hop - 2], vw.at[hop - 1]),
        )
        return [
            pltpu.make_async_remote_copy(
                src_ref=src,
                dst_ref=dst,
                send_sem=send_sems.at[hop - 1, at],
                recv_sem=recv_sems.at[hop - 1, at],
                device_id=right_id,
                device_id_type=pl.DeviceIdType.MESH,
            )
            for at, (src, dst) in enumerate(parts)
        ]

    copies = {hop: hop_copies(hop) for hop in range(1, BACK + 1)}
    copies[1][0].start()
    copies[1][2].start()

    turn = t_ref[...]
    pos = me * rows + lax.broadcasted_iota(jnp.int32, (1, rows), 1)
    count = sp_ref.shape[1]
    first = jnp.transpose(jnp.broadcast_to(sp_ref[0:1, :], (8, count)))[:, 0:1]
    after = jnp.transpose(jnp.broadcast_to(sp_ref[1:2, :], (8, count)))[:, 0:1]
    inside = (pos >= first) & (pos < after)
    tool = jnp.max(jnp.where(inside, 1.0, 0.0), axis=0, keepdims=True)
    ww[0] = jnp.where(tool > 0.5, turn, -1)

    copies[1][1].start()

    def key_block(hops):
        return k_ref if hops == 0 else kw.at[hops - 1]

    def value_block(hops):
        return v_ref if hops == 0 else vw.at[hops - 1]

    hit, one = one_hot_rows(turn, width)
    qc[...] = jnp.transpose(jnp.where(hit | one, 1.0, 0.0)).astype(BF16)

    def prepare(hops):
        w = ww[hops]
        if hops:
            w = jnp.where(me >= hops, w, 1024)
        hit, one = one_hot_rows(w, width)
        code = jnp.where(hit, HIDE, jnp.where(one, -2.0 * HIDE, 0.0))
        code = jnp.where(w >= 0, code, 0.0)
        kc[hops] = jnp.transpose(code).astype(BF16)
        kt[hops] = jnp.transpose(key_block(hops)[...].astype(F32)).astype(BF16)

    def score_part(hops, h, part):
        k0, kn, r0, rn = part
        cols = pl.ds(pl.multiple_of(h * width, width), width)
        k_rows, q_rows = pl.ds(k0, kn), pl.ds(r0, rn)
        keyed = jnp.concatenate([key_block(hops)[k_rows, :], kc[hops, k_rows, :]], axis=1)
        asked = jnp.concatenate([q_s[q_rows, cols], qc[q_rows, :]], axis=1)
        s = dot_nt(keyed, asked)
        dp = dot_nt(value_block(hops)[k_rows, :], do_s[q_rows, cols])
        if hops in (0, BACK):
            key_at = k0 + lax.broadcasted_iota(jnp.int32, (kn, rn), 0)
            row_at = r0 + lax.broadcasted_iota(jnp.int32, (kn, rn), 1)
            seen = key_at <= row_at if hops == 0 else key_at > row_at
            s = jnp.where(seen, s, -2.0 * HIDE)
        top = jnp.max(s, axis=0, keepdims=True) * to_exp2
        if hops:
            before = ms[hops - 1, h, :, q_rows]
            top = jnp.maximum(before, top)
        e = jnp.exp2(s * to_exp2 - top)
        total = jnp.sum(e, axis=0, keepdims=True)
        inner = jnp.sum(e * dp, axis=0, keepdims=True)
        if hops:
            fade = jnp.exp2(before - top)
            total = total + ls[h, :, q_rows] * fade
            inner = inner + dl[h, :, q_rows] * fade
        ms[hops, h, :, q_rows] = top
        ls[h, :, q_rows] = total
        dl[h, :, q_rows] = inner
        es[hops, h, k_rows, q_rows] = e.astype(BF16)
        ds[hops, h, k_rows, q_rows] = dp.astype(BF16)

    def over_heads(step, unroll):
        def body(i, carry):
            for u in range(unroll):
                step(i * unroll + u)
            return carry

        lax.fori_loop(0, heads // unroll, body, 0)

    def score_block(hops):
        def step(h):
            for part in regions(hops, rows):
                score_part(hops, h, part)

        over_heads(step, 8)

    prepare(0)
    q_copy.wait()
    do_copy.wait()
    score_block(0)
    for hops in range(1, BACK + 1):
        for at, copy in enumerate(copies[hops]):
            copy.wait_recv()
            if hops < BACK:
                copies[hops + 1][at].start()
        prepare(hops)
        score_block(hops)

    def finish(h):
        share = 1.0 / ls[h]
        last = ms[BACK, h]
        dl[h] = dl[h] * share
        for hops in range(BACK + 1):
            ms[hops, h] = jnp.exp2(ms[hops, h] - last) * share

    over_heads(finish, 1)

    def grad_part(hops, h, part):
        k0, kn, r0, rn = part
        cols = pl.ds(pl.multiple_of(h * width, width), width)
        k_rows, q_rows = pl.ds(k0, kn), pl.ds(r0, rn)
        p = es[hops, h, k_rows, q_rows].astype(F32) * ms[hops, h, :, q_rows]
        g = p * (ds[hops, h, k_rows, q_rows].astype(F32) - dl[h, :, q_rows])
        p = p.astype(BF16)
        g = g.astype(BF16)
        gk_acc[k_rows, :] += dot(g, q_s[q_rows, cols])
        gv_acc[k_rows, :] += dot(p, do_s[q_rows, cols])
        gq = dot(kt[hops, :, k_rows], g)
        if hops == BACK:
            gq_acc[h, :, q_rows] = gq
        else:
            gq_acc[h, :, q_rows] += gq

    def grad_copies(step):
        return [
            pltpu.make_async_remote_copy(
                src_ref=src.at[step],
                dst_ref=dst.at[step],
                send_sem=gsend_sems.at[step, at],
                recv_sem=grecv_sems.at[step, at],
                device_id=left_id,
                device_id_type=pl.DeviceIdType.MESH,
            )
            for at, (src, dst) in enumerate(((gk_out, gk_in), (gv_out, gv_in)))
        ]

    returns = [grad_copies(step) for step in range(BACK)]

    for step in range(BACK + 1):
        hops = BACK - step
        gk_acc[...] = jnp.zeros_like(gk_acc)
        gv_acc[...] = jnp.zeros_like(gv_acc)

        def grad_step(h):
            for part in regions(hops, rows):
                grad_part(hops, h, part)

        over_heads(grad_step, 4)
        if hops == 0:
            for h in range(heads):
                gq_ref[:, h * width : (h + 1) * width] = (
                    jnp.transpose(gq_acc[h] * scale)
                ).astype(BF16)
        sums = ((gk_acc, gk_in, gk_out, gk_ref, scale), (gv_acc, gv_in, gv_out, gv_ref, 1.0))
        for at, (acc, came, going, result, factor) in enumerate(sums):
            total = acc[...]
            if step:
                returns[step - 1][at].wait_recv()
                total = total + came[step - 1].astype(F32)
            if hops:
                going[step] = total.astype(BF16)
                returns[step][at].start()
            else:
                result[...] = (total * factor).astype(BF16)

    for hop in range(1, BACK + 1):
        for copy in copies[hop]:
            copy.wait_send()
    for step in range(BACK):
        for copy in returns[step]:
            copy.wait_send()


def hand_out(gq_in, gk_in, gv_in, gq_ref, gk_ref, gv_ref):
    gq_ref[...] = gq_in[...]
    gk_ref[...] = gk_in[...]
    gv_ref[...] = gv_in[...]


def on_device(inner_count, device_count, queries, keys, values, grad_out, turn_ids, tool_spans):
    rows, width = keys.shape
    heads = queries.shape[1] // width
    vmem = pl.BlockSpec(memory_space=pltpu.VMEM)
    hbm = pl.BlockSpec(memory_space=pl.ANY)
    block = (rows, width)
    dma = pltpu.SemaphoreType.DMA
    flops = 2 * 5 * heads * rows * (BACK + 1) * rows * width
    parts = pl.pallas_call(
        functools.partial(kernel, inner_count, device_count),
        out_shape=(
            jax.ShapeDtypeStruct(queries.shape, BF16),
            jax.ShapeDtypeStruct(keys.shape, BF16),
            jax.ShapeDtypeStruct(values.shape, BF16),
        ),
        in_specs=[hbm, hbm, vmem, vmem, vmem, vmem],
        out_specs=(vmem, vmem, vmem),
        scratch_shapes=[
            pltpu.VMEM(queries.shape, BF16),
            pltpu.VMEM(queries.shape, BF16),
            pltpu.VMEM((BACK,) + block, BF16),
            pltpu.VMEM((BACK,) + block, BF16),
            pltpu.VMEM((BACK + 1, 1, rows), jnp.int32),
            pltpu.VMEM((BACK + 1,) + block, BF16),
            pltpu.VMEM((BACK + 1, width, rows), BF16),
            pltpu.VMEM(block, BF16),
            pltpu.VMEM((BACK + 1, heads, rows, rows), BF16),
            pltpu.VMEM((BACK + 1, heads, rows, rows), BF16),
            pltpu.VMEM((BACK + 1, heads, 1, rows), F32),
            pltpu.VMEM((heads, 1, rows), F32),
            pltpu.VMEM((heads, 1, rows), F32),
            pltpu.VMEM((heads, width, rows), F32),
            pltpu.VMEM(block, F32),
            pltpu.VMEM(block, F32),
            pltpu.VMEM((BACK,) + block, BF16),
            pltpu.VMEM((BACK,) + block, BF16),
            pltpu.VMEM((BACK,) + block, BF16),
            pltpu.VMEM((BACK,) + block, BF16),
            dma((2,)),
            dma((BACK, 3)),
            dma((BACK, 3)),
            dma((BACK, 2)),
            dma((BACK, 2)),
        ],
        compiler_params=pltpu.CompilerParams(
            collective_id=0, has_side_effects=True, vmem_limit_bytes=60 * 1024 * 1024
        ),
        cost_estimate=pl.CostEstimate(
            flops=flops, bytes_accessed=8 * 1024 * 1024, transcendentals=0
        ),
    )(queries, grad_out, keys, values, turn_ids.reshape(1, rows), tool_spans.T)
    return pl.pallas_call(
        hand_out,
        out_shape=tuple(jax.ShapeDtypeStruct(part.shape, part.dtype) for part in parts),
        in_specs=[vmem, vmem, vmem],
        out_specs=(vmem, vmem, vmem),
        scratch_shapes=[],
    )(*parts)


def solution(mesh):
    placed = (
        P(("outer", "inner"), None),
        P(("outer", "inner"), None),
        P(("outer", "inner"), None),
        P(("outer", "inner"), None),
        P(("outer", "inner")),
        P(),
    )
    return jax.shard_map(
        functools.partial(on_device, mesh.shape["inner"], mesh.size),
        mesh=mesh,
        in_specs=placed,
        out_specs=(
            P(("outer", "inner"), None),
            P(("outer", "inner"), None),
            P(("outer", "inner"), None),
        ),
        check_vma=False,
    )
```
